32 devices in a mesh: chan: 8 (over y, x, core), freq: 4 (over z).
Axes of the slice: x: 2, y: 2, z: 4, core: 2. Of those that a mesh axis runs over, the one named last changes fastest.
Arguments:
- spectra: bfloat16 [2, 2, 192, 1024], P(None, None, 'freq', 'chan'), may hold values from -1000 to 1000
- masks: int32 [2, 1024], P(None, 'chan'), may hold values 0 or 1
- pair_blocks: int32 [48, 2], P('chan'), may hold values from 0 to 7, as said below
Outputs:
- correlations: bfloat16 [48, 201, 128, 128], P('chan', None, 'freq')
The draws below stay inside these ranges and needn't reach their ends.
Inputs may be any that keep to these rules, and one draw needn't show every extreme that they name: `pair_blocks`: row p is owned by block p // 6. Its source block (column 0) and receiver block (column 1) differ, and each lies at most 2 blocks from the owner around the closed loop of blocks. In every draw some row has its source exactly 2 blocks below its owner and its receiver exactly 2 above.
All inputs are finite; a program needn't handle non-finite values. No bound on the sum of `masks` on one device may be relied on, other than what follows from the above.
Results may differ from the reference program's by a relative error of at most 0.0068.
Values may be sent and summed in bfloat16 or wider, within the bound.
A program may use at most 128 MiB of HBM per device.

```python
import math
import jax
import jax.numpy as jnp
from jax import lax

BLK = 128
SEG = 2
PAIR_DEV = 6
REACH = 2
LAGS = 201
CH = 1024
FREQS = 192
PAIRS = 48


def draw_spectra(key, part):
    key = jax.random.fold_in(key, 11)
    base_key, spread_key, chan_key = jax.random.split(key, 3)
    ramp = jnp.arange(FREQS, dtype=jnp.float32) / FREQS
    noise = jnp.clip(jax.random.normal(base_key, (2, SEG, FREQS, CH), jnp.float32), -5.0, 5.0)
    trend = jnp.exp(math.log(3.0) * ramp)
    spread = jnp.exp(jax.random.uniform(spread_key, (FREQS,), jnp.float32, 0.0, math.log(4.0)))
    gains = jnp.exp(jax.random.uniform(chan_key, (SEG, CH), jnp.float32, 0.0, math.log(10.0)))
    field = noise * (trend * spread)[None, None, :, None] * gains[None, :, None, :]
    return field.astype(jnp.bfloat16)


def draw_pair_blocks(key, part):
    key = jax.random.fold_in(key, 23)
    source_key, gap_key, row_key = jax.random.split(key, 3)
    loop_span = 2 * REACH + 1
    block_total = PAIRS // PAIR_DEV
    owners = jnp.arange(PAIRS, dtype=jnp.int32) // PAIR_DEV
    source_off = jax.random.randint(source_key, (PAIRS,), -REACH, REACH + 1, jnp.int32)
    gap_sizes = jax.random.randint(gap_key, (PAIRS,), 1, loop_span, jnp.int32)
    receiver_off = (source_off + REACH + gap_sizes) % loop_span - REACH
    chosen = jax.random.randint(row_key, (), 0, PAIRS, jnp.int32)
    row_ids = jnp.arange(PAIRS, dtype=jnp.int32)
    source_off = jnp.where(row_ids == chosen, -REACH, source_off)
    receiver_off = jnp.where(row_ids == chosen, REACH, receiver_off)
    pair_table = jnp.stack([(owners + source_off) % block_total, (owners + receiver_off) % block_total], axis=1)
    return pair_table.astype(jnp.int32)


def place_ends(entries, key, least, largest):
    shape = entries.shape
    place = [jax.random.randint(jax.random.fold_in(key, axis), (), 0, shape[axis]) for axis in range(len(shape))]
    entries = entries.at[tuple(place)].set(least)
    longest = shape.index(max(shape))
    place[longest] = (place[longest] + 1) % shape[longest]
    return entries.at[tuple(place)].set(largest)


def setup_inputs(seed: int = 0) -> dict:
    splits = jax.random.split(jax.random.key(seed), 4)
    return {
        "spectra": draw_spectra(jax.random.fold_in(splits[3], 71), 0),
        "masks": place_ends((jax.random.randint(splits[1], (SEG, CH), 0, 5) < 4).astype(jnp.int32), jax.random.fold_in(splits[1], 1), 0, 1),
        "pair_blocks": draw_pair_blocks(jax.random.fold_in(splits[3], 71), 0),
    }


epsilon = 1e-06

def lag_table(freq_total, lag_total):
    lag_ids = jnp.arange(lag_total, dtype=jnp.int32) - lag_total // 2
    bin_ids = jnp.arange(freq_total, dtype=jnp.int32)
    phase_index = lag_ids[:, None] * bin_ids[None, :] % (2 * freq_total)
    angles = phase_index.astype(jnp.float32) * (math.pi / freq_total)
    return jnp.concatenate([jnp.cos(angles), -jnp.sin(angles)], axis=1).astype(jnp.bfloat16)

def stacked_cross(source, receiver, source_mask, receiver_mask):
    real_left = jnp.concatenate([source[0], source[1]], axis=0)
    imag_left = jnp.concatenate([source[1], -source[0]], axis=0)
    left_pair = jnp.stack([real_left, imag_left]).astype(jnp.float32)
    right_part = jnp.concatenate([receiver[0], receiver[1]], axis=0).astype(jnp.float32)
    product = jnp.einsum('ckfi,kfj->cfij', left_pair, right_part)
    live_count = jnp.einsum('si,sj->ij', source_mask.astype(jnp.float32), receiver_mask.astype(jnp.float32))
    product = product / jnp.maximum(live_count, 1.0)
    return product.astype(jnp.bfloat16).reshape(2, product.shape[1], -1)

def reference(spectra, masks, pair_blocks):
    values = spectra.astype(jnp.float32)
    energy = lax.optimization_barrier(jnp.sum(values[0] * values[0] + values[1] * values[1], axis=1)) / FREQS
    weights = masks.astype(jnp.float32) / jnp.sqrt(energy + epsilon)
    whitened = (values * weights[None, :, None, :]).astype(jnp.bfloat16)
    lag_cosines = lag_table(FREQS, LAGS)
    root_scale = 1.0 / math.sqrt(FREQS)

    def one_pair(blocks):
        source_start = (blocks[0] * BLK).astype(jnp.int32)
        receiver_start = (blocks[1] * BLK).astype(jnp.int32)
        source = lax.dynamic_slice_in_dim(whitened, source_start, BLK, 3)
        receiver = lax.dynamic_slice_in_dim(whitened, receiver_start, BLK, 3)
        source_mask = lax.dynamic_slice_in_dim(masks, source_start, BLK, 1)
        receiver_mask = lax.dynamic_slice_in_dim(masks, receiver_start, BLK, 1)
        stacked = stacked_cross(source, receiver, source_mask, receiver_mask)
        flattened = stacked.reshape(2 * FREQS, BLK * BLK)
        lagged = jnp.dot(lag_cosines, flattened, preferred_element_type=jnp.float32) * root_scale
        return lagged.reshape(LAGS, BLK, BLK).astype(jnp.bfloat16)
    return lax.map(one_pair, pair_blocks)
```

```python
import functools
import math

import jax
import jax.numpy as jnp
import numpy as np
from jax import lax
from jax.experimental import pallas as pl
from jax.experimental.pallas import tpu as pltpu
from jax.sharding import PartitionSpec as P

REACH = 2
SPAN = 2 * REACH + 1
LAGS = 201
FINE = 8
COARSE = (LAGS + FINE - 1) // FINE
MESH = pl.DeviceIdType.MESH

epsilon = 1e-06


def gather_kernel(chan_count, freq_count, own_ref, mask_ref, near_ref, near_mask_ref,
                  local_sem, send_sem, recv_sem, mask_send_sem, mask_recv_sem):
    bins = own_ref.shape[2]
    me = lax.axis_index("chan")
    row = lax.axis_index("freq")
    sign = 1 - 2 * (me % 2)

    def chan_at(step):
        return (me + step + chan_count) % chan_count

    def freq_at(step):
        return (row + step) % freq_count

    def view(slot, shard):
        return near_ref.at[slot, :, :, pl.ds(pl.multiple_of(shard * bins, 16), bins), :]

    barrier = pltpu.get_barrier_semaphore()
    for step in (-2, -1, 1, 2):
        pl.semaphore_signal(barrier, inc=1, device_id=(chan_at(step), row), device_id_type=MESH)
    for step in range(1, freq_count):
        pl.semaphore_signal(barrier, inc=1, device_id=(me, freq_at(step)), device_id_type=MESH)
    local = pltpu.make_async_copy(own_ref, view(REACH, row), local_sem.at[0])
    local.start()
    local_mask = pltpu.make_async_copy(mask_ref, near_mask_ref.at[REACH], local_sem.at[1])
    local_mask.start()
    pl.semaphore_wait(barrier, 2 * REACH + freq_count - 1)

    sends = []

    def send(source, slot, shard, chan, freq):
        copy = pltpu.make_async_remote_copy(
            src_ref=source,
            dst_ref=view(slot, shard),
            send_sem=send_sem.at[len(sends)],
            recv_sem=recv_sem.at[slot, shard],
            device_id=(chan, freq),
            device_id_type=MESH,
        )
        copy.start()
        sends.append(copy)

    def await_shard(slot, shard):
        pltpu.make_async_remote_copy(
            src_ref=own_ref,
            dst_ref=view(slot, shard),
            send_sem=send_sem.at[0],
            recv_sem=recv_sem.at[slot, shard],
            device_id=(chan_at(1), row),
            device_id_type=MESH,
        ).wait_recv()

    def spread(source, shard):
        send(source, REACH - 2 * sign, shard, chan_at(2 * sign), row)
        send(source, REACH + sign, shard, chan_at(-sign), row)
        send(source, REACH - sign, shard, chan_at(sign), row)

    def relay(shard):
        await_shard(REACH - sign, shard)
        send(view(REACH - sign, shard), REACH - 2 * sign, shard, chan_at(sign), row)

    for step in range(1, freq_count):
        send(own_ref, REACH, row, me, freq_at(step))
    spread(own_ref, row)
    mask_copies = []
    for step in (-2, -1, 1, 2):
        copy = pltpu.make_async_remote_copy(
            src_ref=mask_ref,
            dst_ref=near_mask_ref.at[REACH - step],
            send_sem=mask_send_sem.at[REACH + step],
            recv_sem=mask_recv_sem.at[REACH - step],
            device_id=(chan_at(step), row),
            device_id_type=MESH,
        )
        copy.start()
        mask_copies.append(copy)
    for step in range(1, freq_count):
        shard = freq_at(step)
        await_shard(REACH, shard)
        spread(view(REACH, shard), shard)
        relay(freq_at(step - 1))
    relay(freq_at(freq_count - 1))
    for step in range(freq_count):
        shard = freq_at(step)
        await_shard(REACH + sign, shard)
        await_shard(REACH - 2 * sign, shard)
        await_shard(REACH + 2 * sign, shard)
    for copy in mask_copies:
        copy.wait_recv()
    for copy in mask_copies + sends:
        copy.wait_send()
    local.wait()
    local_mask.wait()


def gather_near(spectra, masks, chan_count, freq_count):
    parts, segments, bins, width = spectra.shape
    any_spec = pl.BlockSpec(memory_space=pl.ANY)
    return pl.pallas_call(
        functools.partial(gather_kernel, chan_count, freq_count),
        out_shape=(
            jax.ShapeDtypeStruct((SPAN, parts, segments, bins * freq_count, width), spectra.dtype),
            jax.ShapeDtypeStruct((SPAN,) + masks.shape, masks.dtype),
        ),
        in_specs=[any_spec, any_spec],
        out_specs=(any_spec, any_spec),
        scratch_shapes=[
            pltpu.SemaphoreType.DMA((2,)),
            pltpu.SemaphoreType.DMA((5 * freq_count - 1,)),
            pltpu.SemaphoreType.DMA((SPAN, freq_count)),
            pltpu.SemaphoreType.DMA((SPAN,)),
            pltpu.SemaphoreType.DMA((SPAN,)),
        ],
        compiler_params=pltpu.CompilerParams(collective_id=0, has_side_effects=True),
        name="gather_near",
    )(spectra, masks)


def correlate_kernel(chan_count, rows, pairs_ref, near_ref, mask_ref, coarse_ref, fine_ref,
                     out_ref, white, fine_wide, turned, count_rows, left, right):
    pair = pl.program_id(0)
    _, parts, segments, bins, width = near_ref.shape
    depth = parts * segments * bins
    half = depth // 2
    me = lax.axis_index("chan")
    row_first = pl.multiple_of(lax.axis_index("freq") * rows, 8)

    @pl.when(pair == 0)
    def _():
        @pl.loop(0, SPAN)
        def _(slot):
            for segment in range(segments):
                real = near_ref[slot, 0, segment].astype(jnp.float32)
                imag = near_ref[slot, 1, segment].astype(jnp.float32)
                energy = jnp.sum(real * real + imag * imag, axis=0, keepdims=True) / bins
                mask = mask_ref[slot, segment : segment + 1, :].astype(jnp.float32)
                weight = mask / jnp.sqrt(energy + epsilon)
                white[slot, 0, segment] = (real * weight).astype(jnp.bfloat16)
                white[slot, 1, segment] = (imag * weight).astype(jnp.bfloat16)

        for step in range(1, FINE):
            for part in range(2):
                column = part * FINE + step
                fine_wide[step, part] = jnp.broadcast_to(
                    fine_ref[:, column : column + 1], (bins, width)
                )

    def slot_of(side):
        return (pairs_ref[pair, side] - me + REACH + chan_count) % chan_count

    source_slot = slot_of(0)
    receiver_slot = slot_of(1)

    source = white[source_slot].reshape(depth, width).astype(jnp.float32)
    turned[...] = source.T
    straight = turned[pl.ds(row_first, rows), :]
    crossed = jnp.concatenate([-straight[:, half:], straight[:, :half]], axis=1)
    for step in range(COARSE):
        mixed = (
            straight * coarse_ref[0, step : step + 1, :]
            + crossed * coarse_ref[1, step : step + 1, :]
        )
        left[step] = mixed.astype(left.dtype)

    live = jnp.zeros((rows, width), jnp.float32)
    for segment in range(segments):
        source_mask = mask_ref[source_slot, segment : segment + 1, :].astype(jnp.float32)
        receiver_mask = mask_ref[receiver_slot, segment : segment + 1, :].astype(jnp.float32)
        count_rows[segment] = jnp.broadcast_to(source_mask, (width, width)).T
        live = live + count_rows[segment, pl.ds(row_first, rows), :] * receiver_mask
    scale = (1.0 / math.sqrt(bins)) / jnp.maximum(live, 1.0)

    for segment in range(segments):
        real = white[receiver_slot, 0, segment]
        imag = white[receiver_slot, 1, segment]
        first = segment * bins
        right[0, first : first + bins, :width] = real
        right[0, half + first : half + first + bins, :width] = imag
        real = real.astype(jnp.float32)
        imag = imag.astype(jnp.float32)
        for step in range(1, FINE):
            cosine = fine_wide[step, 0]
            sine = fine_wide[step, 1]
            lanes = slice((step % 2) * width, (step % 2 + 1) * width)
            right[step // 2, first : first + bins, lanes] = (
                cosine * real + sine * imag
            ).astype(jnp.bfloat16)
            right[step // 2, half + first : half + first + bins, lanes] = (
                cosine * imag - sine * real
            ).astype(jnp.bfloat16)

    @pl.loop(0, FINE // 2)
    def _(fine_pair):
        block = right[fine_pair]
        lhs = left[: COARSE - 1].reshape((COARSE - 1) * rows, depth).astype(jnp.bfloat16)
        product = jnp.dot(lhs, block, preferred_element_type=jnp.float32)
        for step in range(COARSE - 1):
            for side in range(2):
                part = product[step * rows : (step + 1) * rows, side * width : (side + 1) * width]
                out_ref[0, step * FINE + 2 * fine_pair + side] = (part * scale).astype(out_ref.dtype)

    last = jnp.dot(
        left[COARSE - 1].astype(jnp.bfloat16), right[0, :, :width],
        preferred_element_type=jnp.float32,
    )
    out_ref[0, LAGS - 1] = (last * scale).astype(out_ref.dtype)


def angle_tables(bins, repeats):
    ids = np.arange(bins)
    coarse = (np.arange(COARSE)[:, None] * FINE - LAGS // 2) * ids[None, :] % (2 * bins)
    coarse = np.tile(coarse * (math.pi / bins), (1, repeats))
    fine = (np.arange(FINE)[None, :] * ids[:, None]) % (2 * bins) * (math.pi / bins)
    return (
        np.stack([np.cos(coarse), np.sin(coarse)]).astype(np.float32),
        np.concatenate([np.cos(fine), np.sin(fine)], axis=1).astype(np.float32),
    )


def correlate(pair_blocks, near, near_masks, chan_count, rows):
    _, parts, segments, bins, width = near.shape
    depth = parts * segments * bins
    pairs = pair_blocks.shape[0]
    coarse, fine = angle_tables(bins, parts * segments)
    left_type = jnp.bfloat16 if rows % 16 == 0 else jnp.float32
    return pl.pallas_call(
        functools.partial(correlate_kernel, chan_count, rows),
        out_shape=jax.ShapeDtypeStruct((pairs, LAGS, rows, width), jnp.bfloat16),
        grid=(pairs,),
        in_specs=[
            pl.BlockSpec(memory_space=pltpu.SMEM),
            pl.BlockSpec(near.shape, lambda p: (0,) * 5),
            pl.BlockSpec(near_masks.shape, lambda p: (0,) * 3),
            pl.BlockSpec(coarse.shape, lambda p: (0,) * 3),
            pl.BlockSpec(fine.shape, lambda p: (0,) * 2),
        ],
        out_specs=pl.BlockSpec((1, LAGS, rows, width), lambda p: (p, 0, 0, 0)),
        scratch_shapes=[
            pltpu.VMEM(near.shape, jnp.bfloat16),
            pltpu.VMEM((FINE, 2, bins, width), jnp.float32),
            pltpu.VMEM((width, depth), jnp.float32),
            pltpu.VMEM((segments, width, width), jnp.float32),
            pltpu.VMEM((COARSE, rows, depth), left_type),
            pltpu.VMEM((FINE // 2, depth, 2 * width), jnp.bfloat16),
        ],
        compiler_params=pltpu.CompilerParams(
            dimension_semantics=("arbitrary",), vmem_limit_bytes=56 * 1024 * 1024
        ),
        name="correlate",
    )(pair_blocks, near, near_masks, jnp.asarray(coarse), jnp.asarray(fine))


def per_device(chan_count, freq_count, spectra, masks, pair_blocks):
    near, near_masks = gather_near(spectra, masks, chan_count, freq_count)
    rows = spectra.shape[3] // freq_count
    return correlate(pair_blocks, near, near_masks, chan_count, rows)


def solution(mesh):
    return jax.shard_map(
        functools.partial(per_device, mesh.shape["chan"], mesh.shape["freq"]),
        mesh=mesh,
        in_specs=(P(None, None, "freq", "chan"), P(None, "chan"), P("chan", None)),
        out_specs=P("chan", None, "freq", None),
        check_vma=False,
    )
```

```python
import functools
import math

import jax
import jax.numpy as jnp
import numpy as np
from jax import lax
from jax.experimental import pallas as pl
from jax.experimental.pallas import tpu as pltpu
from jax.sharding import PartitionSpec as P

REACH = 2
SPAN = 2 * REACH + 1
LAGS = 201
FINE = 8
FINE_SIDE = FINE // 2
COARSE_SIDE = LAGS // 2 // FINE
COARSE = 2 * COARSE_SIDE + 1
DIRECT = (0, 1)
MESH = pl.DeviceIdType.MESH

epsilon = 1e-06


def gather_kernel(chan_count, freq_count, own_ref, mask_ref, near_ref, near_mask_ref,
                  local_sem, send_sem, recv_sem, mask_send_sem, mask_recv_sem):
    bins = own_ref.shape[2]
    me = lax.axis_index("chan")
    row = lax.axis_index("freq")
    sign = 1 - 2 * (me % 2)

    def chan_at(step):
        return (me + step + chan_count) % chan_count

    def freq_at(step):
        return (row + step) % freq_count

    def view(slot, shard):
        return near_ref.at[slot, :, :, pl.ds(pl.multiple_of(shard * bins, 16), bins), :]

    direct = [step for step in DIRECT if step < freq_count]
    direct += [freq_count - step for step in direct if step not in (0, freq_count - step)]
    barrier = pltpu.get_barrier_semaphore()
    for step in (-2, -1, 1, 2):
        pl.semaphore_signal(barrier, inc=1, device_id=(chan_at(step), row), device_id_type=MESH)
    for step in range(1, freq_count):
        pl.semaphore_signal(barrier, inc=1, device_id=(me, freq_at(step)), device_id_type=MESH)
    for step in direct[1:]:
        for back in (-2 * sign, -sign):
            pl.semaphore_signal(
                barrier, inc=1, device_id=(chan_at(back), freq_at(freq_count - step)),
                device_id_type=MESH,
            )
    local = pltpu.make_async_copy(own_ref, view(REACH, row), local_sem.at[0])
    local.start()
    local_mask = pltpu.make_async_copy(mask_ref, near_mask_ref.at[REACH], local_sem.at[1])
    local_mask.start()
    pl.semaphore_wait(barrier, 2 * REACH + freq_count - 1 + 2 * len(direct[1:]))

    sends = []

    def send(source, slot, shard, chan, freq):
        copy = pltpu.make_async_remote_copy(
            src_ref=source,
            dst_ref=view(slot, shard),
            send_sem=send_sem.at[len(sends)],
            recv_sem=recv_sem.at[slot, shard],
            device_id=(chan, freq),
            device_id_type=MESH,
        )
        copy.start()
        sends.append(copy)

    def await_shard(slot, shard):
        pltpu.make_async_remote_copy(
            src_ref=own_ref,
            dst_ref=view(slot, shard),
            send_sem=send_sem.at[0],
            recv_sem=recv_sem.at[slot, shard],
            device_id=(chan_at(1), row),
            device_id_type=MESH,
        ).wait_recv()

    def spread(source, shard, freq):
        send(source, REACH - 2 * sign, shard, chan_at(2 * sign), freq)
        send(source, REACH + sign, shard, chan_at(-sign), freq)

    def to_partner(source, shard):
        send(source, REACH - sign, shard, chan_at(sign), row)

    def relay(shard):
        await_shard(REACH - sign, shard)
        send(view(REACH - sign, shard), REACH - 2 * sign, shard, chan_at(sign), row)

    chained = [step for step in range(1, freq_count) if step not in direct]
    steps = direct[1:] + chained
    for step in chained + direct[1:]:
        send(own_ref, REACH, row, me, freq_at(step))
    for step in direct:
        spread(own_ref, row, freq_at(step))
    to_partner(own_ref, row)
    mask_copies = []
    for step in (-2, -1, 1, 2):
        copy = pltpu.make_async_remote_copy(
            src_ref=mask_ref,
            dst_ref=near_mask_ref.at[REACH - step],
            send_sem=mask_send_sem.at[REACH + step],
            recv_sem=mask_recv_sem.at[REACH - step],
            device_id=(chan_at(step), row),
            device_id_type=MESH,
        )
        copy.start()
        mask_copies.append(copy)
    for step in chained:
        shard = freq_at(step)
        await_shard(REACH, shard)
        spread(view(REACH, shard), shard, row)
        to_partner(view(REACH, shard), shard)
    relay(row)
    for step in direct[1:]:
        shard = freq_at(step)
        await_shard(REACH, shard)
        to_partner(view(REACH, shard), shard)
    for step in steps:
        relay(freq_at(step))
    for step in range(freq_count):
        shard = freq_at(step)
        await_shard(REACH + sign, shard)
        await_shard(REACH - 2 * sign, shard)
        await_shard(REACH + 2 * sign, shard)
    for copy in mask_copies:
        copy.wait_recv()
    for copy in mask_copies + sends:
        copy.wait_send()
    local.wait()
    local_mask.wait()


def gather_near(spectra, masks, chan_count, freq_count):
    parts, segments, bins, width = spectra.shape
    any_spec = pl.BlockSpec(memory_space=pl.ANY)
    return pl.pallas_call(
        functools.partial(gather_kernel, chan_count, freq_count),
        out_shape=(
            jax.ShapeDtypeStruct((SPAN, parts, segments, bins * freq_count, width), spectra.dtype),
            jax.ShapeDtypeStruct((SPAN,) + masks.shape, masks.dtype),
        ),
        in_specs=[any_spec, any_spec],
        out_specs=(any_spec, any_spec),
        scratch_shapes=[
            pltpu.SemaphoreType.DMA((2,)),
            pltpu.SemaphoreType.DMA((5 * freq_count - 1,)),
            pltpu.SemaphoreType.DMA((SPAN, freq_count)),
            pltpu.SemaphoreType.DMA((SPAN,)),
            pltpu.SemaphoreType.DMA((SPAN,)),
        ],
        compiler_params=pltpu.CompilerParams(collective_id=0, has_side_effects=True),
        name="gather_near",
    )(spectra, masks)


def correlate_kernel(chan_count, rows, pairs_ref, near_ref, mask_ref, coarse_ref, fine_ref,
                     out_ref, white, fine_wide, turned, count_rows, near_scale,
                     left_even, left_odd, right_even, right_odd, beyond_even, beyond_odd):
    pair = pl.program_id(0)
    pairs = pl.num_programs(0)
    _, parts, segments, bins, width = near_ref.shape
    depth = parts * segments * bins
    half = depth // 2
    me = lax.axis_index("chan")
    row_first = pl.multiple_of(lax.axis_index("freq") * rows, 8)

    def slot_of(side, which):
        return (pairs_ref[side, which] - me + REACH + chan_count) % chan_count

    def begin(which, parity):
        source_slot = slot_of(0, which)
        receiver_slot = slot_of(1, which)
        source = white[source_slot].reshape(depth, width).astype(jnp.float32)
        turned[...] = source.T
        live = jnp.zeros((rows, width), jnp.float32)
        for segment in range(segments):
            source_mask = mask_ref[source_slot, segment : segment + 1, :].astype(jnp.float32)
            receiver_mask = mask_ref[receiver_slot, segment : segment + 1, :].astype(jnp.float32)
            count_rows[segment] = jnp.broadcast_to(source_mask, (width, width)).T
            live = live + count_rows[segment, pl.ds(row_first, rows), :] * receiver_mask
        near_scale[parity] = (1.0 / math.sqrt(bins)) / jnp.maximum(live, 1.0)
        return receiver_slot

    def modulate(receiver_slot, left, right, beyond):
        straight = turned[pl.ds(row_first, rows), :]
        crossed = jnp.concatenate([-straight[:, half:], straight[:, :half]], axis=1)
        left[COARSE_SIDE] = straight.astype(left.dtype)
        for step in range(1, COARSE_SIDE + 1):
            cosine = straight * coarse_ref[0, step : step + 1, :]
            sine = crossed * coarse_ref[1, step : step + 1, :]
            left[COARSE_SIDE + step] = (cosine + sine).astype(left.dtype)
            left[COARSE_SIDE - step] = (cosine - sine).astype(left.dtype)
        for segment in range(segments):
            real = white[receiver_slot, 0, segment]
            imag = white[receiver_slot, 1, segment]
            real_rows = slice(segment * bins, (segment + 1) * bins)
            imag_rows = slice(half + segment * bins, half + (segment + 1) * bins)

            def put(fine, new_real, new_imag):
                if fine == FINE_SIDE:
                    beyond[real_rows, :] = new_real.astype(jnp.bfloat16)
                    beyond[imag_rows, :] = new_imag.astype(jnp.bfloat16)
                else:
                    first = (fine + FINE_SIDE) * width
                    right[real_rows, first : first + width] = new_real.astype(jnp.bfloat16)
                    right[imag_rows, first : first + width] = new_imag.astype(jnp.bfloat16)

            put(0, real, imag)
            real = real.astype(jnp.float32)
            imag = imag.astype(jnp.float32)
            for step in range(1, FINE_SIDE + 1):
                cosine = fine_wide[step, 0]
                sine = fine_wide[step, 1]
                real_cosine, real_sine = cosine * real, sine * real
                imag_cosine, imag_sine = cosine * imag, sine * imag
                put(step, real_cosine + imag_sine, imag_cosine - real_sine)
                put(-step, real_cosine - imag_sine, imag_cosine + real_sine)

    def multiply(left, right, beyond, scale):
        lhs = left[...].reshape(COARSE * rows, depth).astype(jnp.bfloat16)
        product = jnp.dot(lhs, right[...], preferred_element_type=jnp.float32)
        for step in range(COARSE):
            for side in range(FINE):
                part = product[step * rows : (step + 1) * rows, side * width : (side + 1) * width]
                out_ref[0, step * FINE + side] = (part * scale).astype(out_ref.dtype)
        last = jnp.dot(
            left[COARSE - 1].astype(jnp.bfloat16), beyond[...],
            preferred_element_type=jnp.float32,
        )
        out_ref[0, LAGS - 1] = (last * scale).astype(out_ref.dtype)

    @pl.when(pair == 0)
    def _():
        @pl.loop(0, SPAN)
        def _(slot):
            for segment in range(segments):
                real = near_ref[slot, 0, segment].astype(jnp.float32)
                imag = near_ref[slot, 1, segment].astype(jnp.float32)
                energy = jnp.sum(real * real + imag * imag, axis=0, keepdims=True) / bins
                mask = mask_ref[slot, segment : segment + 1, :].astype(jnp.float32)
                weight = mask / jnp.sqrt(energy + epsilon)
                white[slot, 0, segment] = (real * weight).astype(jnp.bfloat16)
                white[slot, 1, segment] = (imag * weight).astype(jnp.bfloat16)

        for step in range(1, FINE_SIDE + 1):
            for part in range(2):
                column = part * (FINE_SIDE + 1) + step
                fine_wide[step, part] = jnp.broadcast_to(
                    fine_ref[:, column : column + 1], (bins, width)
                )

        modulate(begin(0, 0), left_even, right_even, beyond_even)

    def one_pair(parity, ours, others):
        receiver_slot = begin(jnp.minimum(pair + 1, pairs - 1), 1 - parity)
        modulate(receiver_slot, *others)
        multiply(*ours, near_scale[parity])

    even = (left_even, right_even, beyond_even)
    odd = (left_odd, right_odd, beyond_odd)

    @pl.when(pair % 2 == 0)
    def _():
        one_pair(0, even, odd)

    @pl.when(pair % 2 == 1)
    def _():
        one_pair(1, odd, even)


def angle_tables(bins, repeats):
    ids = np.arange(bins)
    coarse = np.arange(COARSE_SIDE + 1)[:, None] * FINE * ids[None, :] % (2 * bins)
    coarse = np.tile(coarse * (math.pi / bins), (1, repeats))
    fine = np.arange(FINE_SIDE + 1)[None, :] * ids[:, None] % (2 * bins) * (math.pi / bins)
    return (
        np.stack([np.cos(coarse), np.sin(coarse)]).astype(np.float32),
        np.concatenate([np.cos(fine), np.sin(fine)], axis=1).astype(np.float32),
    )


def correlate(pair_blocks, near, near_masks, chan_count, rows):
    _, parts, segments, bins, width = near.shape
    depth = parts * segments * bins
    pairs = pair_blocks.shape[0]
    coarse, fine = angle_tables(bins, parts * segments)
    left_type = jnp.bfloat16 if rows % 16 == 0 else jnp.float32
    return pl.pallas_call(
        functools.partial(correlate_kernel, chan_count, rows),
        out_shape=jax.ShapeDtypeStruct((pairs, LAGS, rows, width), jnp.bfloat16),
        grid=(pairs,),
        in_specs=[
            pl.BlockSpec(memory_space=pltpu.SMEM),
            pl.BlockSpec(near.shape, lambda p: (0,) * 5),
            pl.BlockSpec(near_masks.shape, lambda p: (0,) * 3),
            pl.BlockSpec(coarse.shape, lambda p: (0,) * 3),
            pl.BlockSpec(fine.shape, lambda p: (0,) * 2),
        ],
        out_specs=pl.BlockSpec((1, LAGS, rows, width), lambda p: (p, 0, 0, 0)),
        scratch_shapes=[
            pltpu.VMEM(near.shape, jnp.bfloat16),
            pltpu.VMEM((FINE_SIDE + 1, 2, bins, width), jnp.float32),
            pltpu.VMEM((width, depth), jnp.float32),
            pltpu.VMEM((segments, width, width), jnp.float32),
            pltpu.VMEM((2, rows, width), jnp.float32),
            pltpu.VMEM((COARSE, rows, depth), left_type),
            pltpu.VMEM((COARSE, rows, depth), left_type),
            pltpu.VMEM((depth, FINE * width), jnp.bfloat16),
            pltpu.VMEM((depth, FINE * width), jnp.bfloat16),
            pltpu.VMEM((depth, width), jnp.bfloat16),
            pltpu.VMEM((depth, width), jnp.bfloat16),
        ],
        compiler_params=pltpu.CompilerParams(
            dimension_semantics=("arbitrary",), vmem_limit_bytes=56 * 1024 * 1024
        ),
        name="correlate",
    )(pair_blocks.T, near, near_masks, jnp.asarray(coarse), jnp.asarray(fine))


def per_device(chan_count, freq_count, spectra, masks, pair_blocks):
    near, near_masks = gather_near(spectra, masks, chan_count, freq_count)
    rows = spectra.shape[3] // freq_count
    return correlate(pair_blocks, near, near_masks, chan_count, rows)


def solution(mesh):
    return jax.shard_map(
        functools.partial(per_device, mesh.shape["chan"], mesh.shape["freq"]),
        mesh=mesh,
        in_specs=(P(None, None, "freq", "chan"), P(None, "chan"), P("chan", None)),
        out_specs=P("chan", None, "freq", None),
        check_vma=False,
    )
```

```python
import functools
import math

import jax
import jax.numpy as jnp
import numpy as np
from jax import lax
from jax.experimental import pallas as pl
from jax.experimental.pallas import tpu as pltpu
from jax.sharding import PartitionSpec as P

REACH = 2
SPAN = 2 * REACH + 1
LAGS = 201
FINE = 8
FINE_SIDE = FINE // 2
COARSE_SIDE = LAGS // 2 // FINE
COARSE = 2 * COARSE_SIDE + 1
DIRECT = (0, 1)
MESH = pl.DeviceIdType.MESH

epsilon = 1e-06


def gather_kernel(chan_count, freq_count, own_ref, mask_ref, near_ref, near_mask_ref,
                  local_sem, send_sem, recv_sem, mask_send_sem, mask_recv_sem):
    bins = own_ref.shape[2]
    me = lax.axis_index("chan")
    row = lax.axis_index("freq")
    sign = 1 - 2 * (me % 2)

    def chan_at(step):
        return (me + step + chan_count) % chan_count

    def freq_at(step):
        return (row + step) % freq_count

    def view(slot, shard):
        return near_ref.at[slot, :, :, pl.ds(pl.multiple_of(shard * bins, 16), bins), :]

    direct = [step for step in DIRECT if step < freq_count]
    direct += [freq_count - step for step in direct if step not in (0, freq_count - step)]
    barrier = pltpu.get_barrier_semaphore()
    for step in (-2, -1, 1, 2):
        pl.semaphore_signal(barrier, inc=1, device_id=(chan_at(step), row), device_id_type=MESH)
    for step in range(1, freq_count):
        pl.semaphore_signal(barrier, inc=1, device_id=(me, freq_at(step)), device_id_type=MESH)
    for step in direct[1:]:
        for back in (-2 * sign, -sign):
            pl.semaphore_signal(
                barrier, inc=1, device_id=(chan_at(back), freq_at(freq_count - step)),
                device_id_type=MESH,
            )
    local = pltpu.make_async_copy(own_ref, view(REACH, row), local_sem.at[0])
    local.start()
    local_mask = pltpu.make_async_copy(mask_ref, near_mask_ref.at[REACH], local_sem.at[1])
    local_mask.start()
    pl.semaphore_wait(barrier, 2 * REACH + freq_count - 1 + 2 * len(direct[1:]))

    sends = []

    def send(source, slot, shard, chan, freq):
        copy = pltpu.make_async_remote_copy(
            src_ref=source,
            dst_ref=view(slot, shard),
            send_sem=send_sem.at[len(sends)],
            recv_sem=recv_sem.at[slot, shard],
            device_id=(chan, freq),
            device_id_type=MESH,
        )
        copy.start()
        sends.append(copy)

    def await_shard(slot, shard):
        pltpu.make_async_remote_copy(
            src_ref=own_ref,
            dst_ref=view(slot, shard),
            send_sem=send_sem.at[0],
            recv_sem=recv_sem.at[slot, shard],
            device_id=(chan_at(1), row),
            device_id_type=MESH,
        ).wait_recv()

    def spread(source, shard, freq):
        send(source, REACH - 2 * sign, shard, chan_at(2 * sign), freq)
        send(source, REACH + sign, shard, chan_at(-sign), freq)

    def to_partner(source, shard):
        send(source, REACH - sign, shard, chan_at(sign), row)

    def relay(shard):
        await_shard(REACH - sign, shard)
        send(view(REACH - sign, shard), REACH - 2 * sign, shard, chan_at(sign), row)

    chained = [step for step in range(1, freq_count) if step not in direct]
    steps = direct[1:] + chained
    for step in chained + direct[1:]:
        send(own_ref, REACH, row, me, freq_at(step))
    for step in direct:
        spread(own_ref, row, freq_at(step))
    to_partner(own_ref, row)
    mask_copies = []
    for step in (-2, -1, 1, 2):
        copy = pltpu.make_async_remote_copy(
            src_ref=mask_ref,
            dst_ref=near_mask_ref.at[REACH - step],
            send_sem=mask_send_sem.at[REACH + step],
            recv_sem=mask_recv_sem.at[REACH - step],
            device_id=(chan_at(step), row),
            device_id_type=MESH,
        )
        copy.start()
        mask_copies.append(copy)
    for step in chained:
        shard = freq_at(step)
        await_shard(REACH, shard)
        spread(view(REACH, shard), shard, row)
        to_partner(view(REACH, shard), shard)
    relay(row)
    for step in direct[1:]:
        shard = freq_at(step)
        await_shard(REACH, shard)
        to_partner(view(REACH, shard), shard)
    for step in steps:
        relay(freq_at(step))
    for step in range(freq_count):
        shard = freq_at(step)
        await_shard(REACH + sign, shard)
        await_shard(REACH - 2 * sign, shard)
        await_shard(REACH + 2 * sign, shard)
    for copy in mask_copies:
        copy.wait_recv()
    for copy in mask_copies + sends:
        copy.wait_send()
    local.wait()
    local_mask.wait()


def gather_near(spectra, masks, chan_count, freq_count):
    parts, segments, bins, width = spectra.shape
    any_spec = pl.BlockSpec(memory_space=pl.ANY)
    return pl.pallas_call(
        functools.partial(gather_kernel, chan_count, freq_count),
        out_shape=(
            jax.ShapeDtypeStruct((SPAN, parts, segments, bins * freq_count, width), spectra.dtype),
            jax.ShapeDtypeStruct((SPAN,) + masks.shape, masks.dtype),
        ),
        in_specs=[any_spec, any_spec],
        out_specs=(any_spec, any_spec),
        scratch_shapes=[
            pltpu.SemaphoreType.DMA((2,)),
            pltpu.SemaphoreType.DMA((5 * freq_count - 1,)),
            pltpu.SemaphoreType.DMA((SPAN, freq_count)),
            pltpu.SemaphoreType.DMA((SPAN,)),
            pltpu.SemaphoreType.DMA((SPAN,)),
        ],
        compiler_params=pltpu.CompilerParams(collective_id=0, has_side_effects=True),
        name="gather_near",
    )(spectra, masks)


def correlate_kernel(chan_count, rows, pairs_ref, near_ref, mask_ref, coarse_ref, fine_ref,
                     out_ref, white, fine_wide, turned, count_rows, near_scale,
                     left_even, left_odd, right_even, right_odd, beyond_even, beyond_odd):
    pair = pl.program_id(0)
    pairs = pl.num_programs(0)
    _, parts, segments, bins, width = near_ref.shape
    depth = parts * segments * bins
    half = depth // 2
    me = lax.axis_index("chan")
    row_first = pl.multiple_of(lax.axis_index("freq") * rows, 8)

    def slot_of(side, which):
        return (pairs_ref[side, which] - me + REACH + chan_count) % chan_count

    def begin(which, parity):
        source_slot = slot_of(0, which)
        receiver_slot = slot_of(1, which)
        source = white[source_slot].reshape(depth, width).astype(jnp.float32)
        turned[...] = source.T
        live = jnp.zeros((rows, width), jnp.float32)
        for segment in range(segments):
            source_mask = mask_ref[source_slot, segment : segment + 1, :].astype(jnp.float32)
            receiver_mask = mask_ref[receiver_slot, segment : segment + 1, :].astype(jnp.float32)
            count_rows[segment] = jnp.broadcast_to(source_mask, (width, width)).T
            live = live + count_rows[segment, pl.ds(row_first, rows), :] * receiver_mask
        near_scale[parity] = (1.0 / math.sqrt(bins)) / jnp.maximum(live, 1.0)
        return receiver_slot

    def modulate(receiver_slot, left, right, beyond):
        straight = turned[pl.ds(row_first, rows), :]
        crossed = jnp.concatenate([-straight[:, half:], straight[:, :half]], axis=1)
        left[COARSE_SIDE] = straight.astype(left.dtype)
        for step in range(1, COARSE_SIDE + 1):
            cosine = straight * coarse_ref[0, step : step + 1, :]
            sine = crossed * coarse_ref[1, step : step + 1, :]
            left[COARSE_SIDE + step] = (cosine + sine).astype(left.dtype)
            left[COARSE_SIDE - step] = (cosine - sine).astype(left.dtype)
        for segment in range(segments):
            real = white[receiver_slot, 0, segment]
            imag = white[receiver_slot, 1, segment]
            real_rows = slice(segment * bins, (segment + 1) * bins)
            imag_rows = slice(half + segment * bins, half + (segment + 1) * bins)

            def put(fine, new_real, new_imag):
                if fine == FINE_SIDE:
                    beyond[real_rows, :] = new_real.astype(jnp.bfloat16)
                    beyond[imag_rows, :] = new_imag.astype(jnp.bfloat16)
                else:
                    first = (fine + FINE_SIDE) * width
                    right[real_rows, first : first + width] = new_real.astype(jnp.bfloat16)
                    right[imag_rows, first : first + width] = new_imag.astype(jnp.bfloat16)

            put(0, real, imag)
            real = real.astype(jnp.float32)
            imag = imag.astype(jnp.float32)
            for step in range(1, FINE_SIDE + 1):
                cosine = fine_wide[step, 0]
                sine = fine_wide[step, 1]
                real_cosine, real_sine = cosine * real, sine * real
                imag_cosine, imag_sine = cosine * imag, sine * imag
                put(step, real_cosine + imag_sine, imag_cosine - real_sine)
                put(-step, real_cosine - imag_sine, imag_cosine + real_sine)

    def multiply(left, right, beyond, scale):
        lhs = left[...].reshape(COARSE * rows, depth).astype(jnp.bfloat16)
        product = jnp.dot(lhs, right[...], preferred_element_type=jnp.float32)
        for step in range(COARSE):
            for side in range(FINE):
                part = product[step * rows : (step + 1) * rows, side * width : (side + 1) * width]
                out_ref[0, step * FINE + side] = (part * scale).astype(out_ref.dtype)
        last = jnp.dot(
            left[COARSE - 1].astype(jnp.bfloat16), beyond[...],
            preferred_element_type=jnp.float32,
        )
        out_ref[0, LAGS - 1] = (last * scale).astype(out_ref.dtype)

    @pl.when(pair == 0)
    def _():
        @pl.loop(0, SPAN)
        def _(slot):
            for segment in range(segments):
                real = near_ref[slot, 0, segment].astype(jnp.float32)
                imag = near_ref[slot, 1, segment].astype(jnp.float32)
                energy = jnp.sum(real * real + imag * imag, axis=0, keepdims=True) / bins
                mask = mask_ref[slot, segment : segment + 1, :].astype(jnp.float32)
                weight = mask / jnp.sqrt(energy + epsilon)
                white[slot, 0, segment] = (real * weight).astype(jnp.bfloat16)
                white[slot, 1, segment] = (imag * weight).astype(jnp.bfloat16)

        for step in range(1, FINE_SIDE + 1):
            for part in range(2):
                column = part * (FINE_SIDE + 1) + step
                fine_wide[step, part] = jnp.broadcast_to(
                    fine_ref[:, column : column + 1], (bins, width)
                )

        modulate(begin(0, 0), left_even, right_even, beyond_even)

    def one_pair(parity, ours, others):
        @pl.when(pair + 1 < pairs)
        def _():
            modulate(begin(pair + 1, 1 - parity), *others)

        multiply(*ours, near_scale[parity])

    even = (left_even, right_even, beyond_even)
    odd = (left_odd, right_odd, beyond_odd)

    @pl.when(pair % 2 == 0)
    def _():
        one_pair(0, even, odd)

    @pl.when(pair % 2 == 1)
    def _():
        one_pair(1, odd, even)


def angle_tables(bins, repeats):
    ids = np.arange(bins)
    coarse = np.arange(COARSE_SIDE + 1)[:, None] * FINE * ids[None, :] % (2 * bins)
    coarse = np.tile(coarse * (math.pi / bins), (1, repeats))
    fine = np.arange(FINE_SIDE + 1)[None, :] * ids[:, None] % (2 * bins) * (math.pi / bins)
    return (
        np.stack([np.cos(coarse), np.sin(coarse)]).astype(np.float32),
        np.concatenate([np.cos(fine), np.sin(fine)], axis=1).astype(np.float32),
    )


def correlate(pair_blocks, near, near_masks, chan_count, rows):
    _, parts, segments, bins, width = near.shape
    depth = parts * segments * bins
    pairs = pair_blocks.shape[0]
    coarse, fine = angle_tables(bins, parts * segments)
    left_type = jnp.bfloat16 if rows % 16 == 0 else jnp.float32
    return pl.pallas_call(
        functools.partial(correlate_kernel, chan_count, rows),
        out_shape=jax.ShapeDtypeStruct((pairs, LAGS, rows, width), jnp.bfloat16),
        grid=(pairs,),
        in_specs=[
            pl.BlockSpec(memory_space=pltpu.SMEM),
            pl.BlockSpec(near.shape, lambda p: (0,) * 5),
            pl.BlockSpec(near_masks.shape, lambda p: (0,) * 3),
            pl.BlockSpec(coarse.shape, lambda p: (0,) * 3),
            pl.BlockSpec(fine.shape, lambda p: (0,) * 2),
        ],
        out_specs=pl.BlockSpec((1, LAGS, rows, width), lambda p: (p, 0, 0, 0)),
        scratch_shapes=[
            pltpu.VMEM(near.shape, jnp.bfloat16),
            pltpu.VMEM((FINE_SIDE + 1, 2, bins, width), jnp.float32),
            pltpu.VMEM((width, depth), jnp.float32),
            pltpu.VMEM((segments, width, width), jnp.float32),
            pltpu.VMEM((2, rows, width), jnp.float32),
            pltpu.VMEM((COARSE, rows, depth), left_type),
            pltpu.VMEM((COARSE, rows, depth), left_type),
            pltpu.VMEM((depth, FINE * width), jnp.bfloat16),
            pltpu.VMEM((depth, FINE * width), jnp.bfloat16),
            pltpu.VMEM((depth, width), jnp.bfloat16),
            pltpu.VMEM((depth, width), jnp.bfloat16),
        ],
        compiler_params=pltpu.CompilerParams(
            dimension_semantics=("arbitrary",), vmem_limit_bytes=56 * 1024 * 1024
        ),
        name="correlate",
    )(pair_blocks.T, near, near_masks, jnp.asarray(coarse), jnp.asarray(fine))


def per_device(chan_count, freq_count, spectra, masks, pair_blocks):
    near, near_masks = gather_near(spectra, masks, chan_count, freq_count)
    rows = spectra.shape[3] // freq_count
    return correlate(pair_blocks, near, near_masks, chan_count, rows)


def solution(mesh):
    return jax.shard_map(
        functools.partial(per_device, mesh.shape["chan"], mesh.shape["freq"]),
        mesh=mesh,
        in_specs=(P(None, None, "freq", "chan"), P(None, "chan"), P("chan", None)),
        out_specs=P("chan", None, "freq", None),
        check_vma=False,
    )
```
